32 devices in a mesh: wide: 8 (over y, x, core), narrow: 4 (over z).
Axes of the slice: x: 2, y: 2, z: 4, core: 2. Of those that a mesh axis runs over, the one named last changes fastest.
Arguments:
- documents: bfloat16 [8192, 768], P('wide'), may hold values from -8 to 8
- label_weight: bfloat16 [4096, 768], P(('wide', 'narrow')), may hold values from -1 to 1
- sample_ids: int32 [4096], P(('wide', 'narrow')), may hold values from 0 to 2812280, as said below
- positive_cols: int32 [8192, 4], P('wide'), may hold values from 0 to 4095
- up_weight: bfloat16 [768, 3072], P(None, 'narrow'), may hold values from -0.21875 to 0.21875
- down_weight: bfloat16 [3072, 768], P('narrow'), may hold values from -0.109375 to 0.109375
Outputs:
- label_grad: float32 [4096, 768], P(('wide', 'narrow'))
- up_grad: float32 [768, 3072], P('wide', 'narrow')
- down_grad: float32 [3072, 768], P('narrow', 'wide')
The draws below stay inside these ranges and needn't reach their ends.
Inputs may be any that keep to these rules, and one draw needn't show every extreme that they name: `sample_ids`: frequency ranks (0 is the most frequent of 2812281 labels), not falling along the sampled columns; frequent ranks repeat.
All inputs are finite; a program needn't handle non-finite values.
Results may differ from the reference program's by a relative error of at most 0.01.
Values may be sent and summed in bfloat16 or wider, within the bound.
A program may use at most 64 MiB of HBM per device.

```python
import math
from functools import partial
import jax
import jax.numpy as jnp
from jax import lax

D = 768
FF = 3072
CATALOG = 2812281
POS_DOC = 4
DOC_DEV = 1024
B = 8192
S = 4096


def rank_draw(key):
    key_expo, key_rank = jax.random.split(jax.random.fold_in(key, 5113))
    expo = jax.random.randint(key_expo, (S,), 0, 23)
    raw = jax.random.randint(key_rank, (S,), 0, jnp.left_shift(jnp.int32(1), expo))
    return jnp.sort(jnp.minimum(raw, CATALOG - 1))


def expected_log_drawn(rank_ids):
    rank_float = rank_ids.astype(jnp.float32)
    return jnp.log(jnp.float32(S)) + jnp.log(jnp.log1p(1.0 / (rank_float + 1.0))) - jnp.log(jnp.log(jnp.float32(CATALOG) + 1.0))


def draw_sample_ids(key, part):
    return rank_draw(key)


def draw_documents(key, part):
    key_base, key_scale = jax.random.split(jax.random.fold_in(key, 1201))
    base = jnp.clip(jax.random.normal(key_base, (B, D), jnp.float32), -4.0, 4.0)
    row_scale = jnp.exp(jax.random.uniform(key_scale, (B, 1), jnp.float32, math.log(0.5), math.log(2.0)))
    values = base * row_scale
    values = values.at[:, 0].set(8.0)
    return values.astype(jnp.bfloat16)


def draw_label_weight(key, part):
    key_base, key_scale = jax.random.split(jax.random.fold_in(key, 3307))
    base = jnp.clip(jax.random.normal(key_base, (S, D), jnp.float32), -4.0, 4.0)
    row_scale = jnp.exp(jax.random.uniform(key_scale, (S, 1), jnp.float32, math.log(0.5), math.log(2.0)))
    weights = base * row_scale * (1.5 / math.sqrt(D))
    first_column = jnp.clip(expected_log_drawn(rank_draw(key)) / 8.0, -1.0, 1.0)
    weights = weights.at[:, 0].set(first_column)
    return weights.astype(jnp.bfloat16)


def set_ends(values, rng, smallest, top_value):
    longest = values.shape.index(max(values.shape))
    spots = []
    for shift in (0, 1):
        where = [jax.random.randint(jax.random.fold_in(rng, axis), (), 0, length) for axis, length in enumerate(values.shape)]
        where[longest] = (where[longest] + shift) % values.shape[longest]
        spots.append(tuple(where))
    return values.at[spots[0]].set(smallest).at[spots[1]].set(top_value)


def levels(own_key, dims, cuts, smallest, high):
    loudness, own = 1.0, jax.random.fold_in(own_key, 6)
    for position, blocks in cuts:
        heights = jnp.exp(jax.random.uniform(jax.random.fold_in(own, position), (blocks,), jnp.float32, smallest / len(cuts), high / len(cuts)))
        loudness = loudness * jnp.repeat(heights, dims[position] // blocks).reshape([-1 if axis == position else 1 for axis in range(len(dims))])
    return loudness


def bell_draw(key, shape, width, bound, shards=(), kind=jnp.bfloat16):
    result = jax.random.normal(key, shape, jnp.float32) * width
    if len(shards) > 0:
        result = levels(key, shape, shards, -0.22, 0.18) * result
    return jnp.clip(result, min=-bound, max=bound).astype(kind)


def setup_inputs(seed: int = 0) -> dict:
    key_of = jax.random.split(jax.random.key(seed), 7)
    documents = draw_documents(jax.random.fold_in(key_of[6], 71), 0)
    label_weight = draw_label_weight(jax.random.fold_in(key_of[6], 71), 0)
    sample_ids = draw_sample_ids(jax.random.fold_in(key_of[6], 71), 0)
    positive_cols = set_ends(jax.random.randint(key_of[3], (B, POS_DOC), 0, S), jax.random.fold_in(key_of[3], 1), 0, S - 1).astype(jnp.int32)
    up_weight = bell_draw(key_of[4], (D, FF), D ** -0.5, 0.21875, ((1, 4),))
    down_weight = bell_draw(key_of[5], (FF, D), FF ** -0.5, 0.109375, ((0, 4),))
    return {"documents": documents, "label_weight": label_weight, "sample_ids": sample_ids, "positive_cols": positive_cols, "up_weight": up_weight, "down_weight": down_weight}


def expected_log(rank_ids, sampled):
    rank_float = rank_ids.astype(jnp.float32)
    return jnp.log(jnp.float32(sampled)) + jnp.log(jnp.log1p(1.0 / (rank_float + 1.0))) - jnp.log(jnp.log(jnp.float32(CATALOG) + 1.0))

def reference(documents, label_weight, sample_ids, positive_cols, up_weight, down_weight):
    log_expect = expected_log(sample_ids, S)
    pre_act = jnp.dot(documents, up_weight, preferred_element_type=jnp.float32)
    hidden = jax.nn.gelu(pre_act, approximate=False).astype(jnp.bfloat16)
    summed = jnp.dot(hidden, down_weight, preferred_element_type=jnp.float32)
    embedding = (documents.astype(jnp.float32) + summed).astype(jnp.bfloat16)
    groups = B // DOC_DEV
    doc_blocks = embedding.reshape(groups, DOC_DEV, D)
    pos_blocks = positive_cols.reshape(groups, DOC_DEV, POS_DOC)
    row_index = jnp.arange(DOC_DEV, dtype=jnp.int32)[:, None]

    def one_group(label_acc, block_item):
        doc_block, pos_block = block_item
        logits = jnp.dot(doc_block, label_weight.T, preferred_element_type=jnp.float32) - log_expect[None, :]
        row_top = lax.optimization_barrier(jnp.max(logits, axis=1, keepdims=True))
        log_total = row_top + jnp.log(lax.optimization_barrier(jnp.sum(jnp.exp(logits - row_top), axis=1, keepdims=True)))
        positive_hits = jnp.zeros(logits.shape, jnp.float32).at[row_index, pos_block].add(1.0)
        grad_logits = (jnp.exp(logits - log_total) - positive_hits / POS_DOC).astype(jnp.bfloat16)
        embed_back = jnp.dot(grad_logits, label_weight, preferred_element_type=jnp.float32)
        label_acc = label_acc + jnp.dot(grad_logits.T, doc_block, preferred_element_type=jnp.float32)
        return (label_acc, embed_back)
    label_grad, embed_back = lax.scan(one_group, jnp.zeros((S, D), jnp.float32), (doc_blocks, pos_blocks))
    embed_grad = embed_back.reshape(B, D).astype(jnp.bfloat16)
    act_grad = jnp.dot(embed_grad, down_weight.T, preferred_element_type=jnp.float32)
    _, gelu_pull = jax.vjp(partial(jax.nn.gelu, approximate=False), pre_act)
    pre_grad = gelu_pull(act_grad)[0].astype(jnp.bfloat16)
    down_grad = jnp.dot(hidden.T, embed_grad, preferred_element_type=jnp.float32)
    up_grad = jnp.dot(documents.T, pre_grad, preferred_element_type=jnp.float32)
    return (label_grad, up_grad, down_grad)
```

```python
import functools

import jax
import jax.numpy as jnp
from jax import lax
from jax.experimental import pallas as pl
from jax.experimental.pallas import tpu as pltpu
from jax.sharding import PartitionSpec as P

CATALOG = 2812281
MESH = pl.DeviceIdType.MESH
F32 = jnp.float32
BF16 = jnp.bfloat16
CHUNK = 256
PIECE = 64
LAG = 2
NN = (((1,), (0,)), ((), ()))
NT = (((1,), (1,)), ((), ()))
TN = (((0,), (0,)), ((), ()))


def dot(a, b, dims):
    return lax.dot_general(a, b, dims, preferred_element_type=F32)


def kernel(
    nw, nn, per_doc,
    docs, label, log_exp, pos, up, down,
    label_out, up_out, down_out,
    labels, log_all, log_col, hidden, slope, own, emb, expo, grad, stat, stat_all,
    up_in, up_send, dn_in, dn_send, up_in2, up_send2, dn_in2, dn_send2,
    own2, embed_grad, label_acc, label_send, label_recv, up_acc, down_acc, pair_send, pair_recv,
    final_send, final_recv,
    g_send, g_recv, l_send, l_recv, s_send, s_recv,
    us_sem, ur_sem, ds_sem, dr_sem, us2_sem, ur2_sem, ds2_sem, dr2_sem,
    hs_sem, hr_sem, ps_sem, pr_sem, fs_sem, fr_sem,
):
    rows = docs.shape[0]
    lab = label.shape[0]
    chunks, pieces = rows // CHUNK, rows // PIECE
    per_chunk = CHUNK // PIECE
    wide = lax.axis_index("wide")
    me = lax.axis_index("narrow")

    barrier = pltpu.get_barrier_semaphore()

    @pl.loop(1, nw)
    def _(r):
        pl.semaphore_signal(barrier, inc=1, device_id={"wide": lax.rem(wide + r, nw)}, device_id_type=MESH)

    @pl.loop(1, nn)
    def _(r):
        pl.semaphore_signal(barrier, inc=1, device_id={"narrow": lax.rem(me + r, nn)}, device_id_type=MESH)

    pl.semaphore_wait(barrier, nw + nn - 2)

    def remote(src, dst, send, recv, **device):
        return pltpu.make_async_remote_copy(
            src_ref=src, dst_ref=dst, send_sem=send, recv_sem=recv, device_id=device, device_id_type=MESH
        )

    def label_copy(r):
        return remote(label, labels.at[pl.ds(pl.multiple_of(wide * lab, lab), lab)], g_send.at[r], g_recv.at[wide],
                      wide=lax.rem(wide + r, nw))

    def log_copy(r):
        return remote(log_exp, log_all.at[wide], l_send.at[r], l_recv.at[wide], wide=lax.rem(wide + r, nw))

    @pl.loop(1, nw)
    def _(r):
        log_copy(r).start()
        label_copy(r).start()

    labels[pl.ds(pl.multiple_of(wide * lab, lab), lab), :] = label[...]
    log_all[wide] = log_exp[...]

    def chunk_of(c):
        return pl.ds(pl.multiple_of(c * CHUNK, CHUNK), CHUNK)

    def piece_of(p):
        return pl.ds(pl.multiple_of(p * PIECE, PIECE), PIECE)

    def forward(c):
        at = chunk_of(c)
        pre = dot(docs[at, :], up[...], NN)
        cdf = 0.5 * (1.0 + lax.erf(pre * 0.7071067811865476))
        slope[at, :] = cdf + pre * jnp.exp(-0.5 * pre * pre) * 0.3989422804014327
        mid = (pre * cdf).astype(BF16)
        hidden[at, :] = mid
        own[at, :] = dot(mid, down[...], NN)

    def scan_step(t, terms, u_in, u_send, d_in, d_send, us, ur, ds, dr, finish):
        def one(p, first, last, inbox, outbox, send, recv, target):
            at = piece_of(p)

            @pl.when((p >= 0) & (p < pieces))
            def _():
                @pl.when(jnp.logical_not(first))
                def _():
                    remote(outbox.at[at], inbox.at[at], send.at[p], recv.at[p], narrow=target).wait_recv()

                @pl.when(jnp.logical_not(last))
                def _():
                    @pl.when(first)
                    def _():
                        outbox[at, :] = terms[at, :].astype(BF16)

                    @pl.when(jnp.logical_not(first))
                    def _():
                        outbox[at, :] = (terms[at, :] + inbox[at, :].astype(F32)).astype(BF16)

                    remote(outbox.at[at], inbox.at[at], send.at[p], recv.at[p], narrow=target).start()

        low, high = me == 0, me == nn - 1
        one(t - LAG * me, low, high, u_in, u_send, us, ur, lax.rem(me + 1, nn))
        one(t - LAG * (nn - 1 - me), high, low, d_in, d_send, ds, dr, lax.rem(me + nn - 1, nn))
        q = t - LAG * jnp.maximum(me, nn - 1 - me)
        at = piece_of(q)

        @pl.when((q >= 0) & (q < pieces))
        def _():
            @pl.when(low)
            def _():
                finish(at, terms[at, :] + d_in[at, :].astype(F32))

            @pl.when(high)
            def _():
                finish(at, terms[at, :] + u_in[at, :].astype(F32))

            @pl.when(jnp.logical_not(low | high))
            def _():
                finish(at, terms[at, :] + u_in[at, :].astype(F32) + d_in[at, :].astype(F32))

        return q

    def drain(outbox, inbox, send, recv, skip):
        @pl.when(jnp.logical_not(skip))
        def _():
            @pl.loop(0, pieces)
            def _(p):
                at = piece_of(p)
                remote(outbox.at[at], inbox.at[at], send.at[p], recv.at[p], narrow=lax.rem(me + 1, nn)).wait_send()

    def when_chunk(q, act):
        done = (q >= 0) & (q < pieces) & (lax.rem(q + pieces, per_chunk) == per_chunk - 1)

        @pl.when(done)
        def _():
            act(q // per_chunk)

    def tile(w):
        return pl.ds(pl.multiple_of(w * lab, lab), lab)

    def stat_copy(r, c):
        return remote(stat.at[c], stat_all.at[me, c], s_send.at[r, c], s_recv.at[me, c], narrow=lax.rem(me + r, nn))

    def logits(c):
        @pl.when(c == 0)
        def _():
            @pl.loop(1, nw)
            def _(r):
                src = lax.rem(wide + r, nw)
                remote(label, labels.at[tile(src)], g_send.at[r], g_recv.at[src], wide=src).wait_recv()
                remote(log_exp, log_all.at[src], l_send.at[r], l_recv.at[src], wide=src).wait_recv()

            @pl.loop(0, nw)
            def _(w):
                log_col[tile(w), :] = jnp.broadcast_to(log_all[w][0:1, :], (lab, lab)).T

        expo[c] = dot(labels[...], emb[chunk_of(c), :], NT)

        def top(w, best):
            part = expo[c, tile(w), :] - log_col[tile(w), 0:1]
            expo[c, tile(w), :] = part
            return jnp.maximum(best, jnp.max(part, axis=0, keepdims=True))

        best = lax.fori_loop(0, nw, top, jnp.full((1, CHUNK), -jnp.inf, F32))

        def add(w, total):
            part = jnp.exp(expo[c, tile(w), :] - best)
            expo[c, tile(w), :] = part
            return total + jnp.sum(part, axis=0, keepdims=True)

        total = lax.fori_loop(0, nw, add, jnp.zeros((1, CHUNK), F32))
        stat[c, 0:1, :] = best
        stat[c, 1:2, :] = total

        @pl.loop(1, nn)
        def _(r):
            stat_copy(r, c).start()

    def finish_embedding(at, value):
        emb[at, :] = (docs[at, :].astype(F32) + value).astype(BF16)

    steps = pieces + LAG * (nn - 1)
    stat[...] = jnp.zeros_like(stat)
    forward(0)

    @pl.loop(0, steps)
    def _(t):
        q = scan_step(t, own, up_in, up_send, dn_in, dn_send, us_sem, ur_sem, ds_sem, dr_sem, finish_embedding)

        @pl.when(t < chunks - 1)
        def _():
            forward(t + 1)

        when_chunk(q, logits)

    def gradient(c):
        @pl.loop(1, nn)
        def _(r):
            src = lax.rem(me + r, nn)
            remote(stat.at[c], stat_all.at[src, c], s_send.at[r, c], s_recv.at[src, c], narrow=src).wait_recv()

        mine, mine_sum = stat[c, 0:1, :], stat[c, 1:2, :]
        top = lax.fori_loop(
            1, nn, lambda r, m: jnp.maximum(m, stat_all[lax.rem(me + r, nn), c, 0:1, :]), mine
        )

        def add(r, s):
            src = lax.rem(me + r, nn)
            return s + stat_all[src, c, 1:2, :] * jnp.exp(stat_all[src, c, 0:1, :] - top)

        shrink = jnp.exp(mine - top)
        scale = shrink / lax.fori_loop(1, nn, add, mine_sum * shrink)
        offsets = lax.broadcasted_iota(jnp.int32, (lab, CHUNK), 0)

        @pl.loop(0, nw)
        def _(w):
            columns = offsets + (w * nn + me) * lab
            hits = jnp.zeros((lab, CHUNK), F32)
            for k in range(per_doc):
                hits = hits + jnp.where(pos[c, k : k + 1, :] == columns, 1.0, 0.0)
            grad[tile(w), :] = (expo[c, tile(w), :] * scale - hits / per_doc).astype(BF16)

        own2[chunk_of(c), :] = dot(grad[...], labels[...], TN)

    def label_part(c):
        label_acc[...] += dot(grad[...], emb[chunk_of(c), :], NN)

    def home_copy(r):
        to = lax.rem(wide + r, nw)
        return remote(label_send.at[tile(to)], label_recv.at[tile(wide)], hs_sem.at[r], hr_sem.at[wide], wide=to)

    def finish_gradient(at, value):
        embed_grad[at, :] = value.astype(BF16)

    def backward(c):
        at = chunk_of(c)
        back = embed_grad[at, :]
        pre_grad = (dot(back, down[...], NT) * slope[at, :]).astype(BF16)
        up_acc[...] += dot(docs[at, :], pre_grad, TN)
        down_acc[...] += dot(back, hidden[at, :], TN)

    label_acc[...] = jnp.zeros_like(label_acc)
    up_acc[...] = jnp.zeros_like(up_acc)
    down_acc[...] = jnp.zeros_like(down_acc)
    gradient(0)

    @pl.loop(0, steps)
    def _(t):
        q = scan_step(
            t, own2, up_in2, up_send2, dn_in2, dn_send2, us2_sem, ur2_sem, ds2_sem, dr2_sem, finish_gradient
        )

        @pl.when(t < chunks)
        def _():
            label_part(t)

        @pl.when(t < chunks - 1)
        def _():
            gradient(t + 1)

        @pl.when(t == chunks - 1)
        def _():
            label_send[...] = label_acc[...].astype(BF16)

            @pl.loop(1, nw)
            def _(r):
                home_copy(r).start()

        when_chunk(q, backward)

    blk = up_acc.shape[0] // nw
    half = nw // 2
    side = lax.rem(wide, 2)
    other = wide + 1 - 2 * side

    def block(b):
        return pl.ds(pl.multiple_of(b * blk, blk), blk)

    def pair_copy(i):
        return remote(pair_send.at[i], pair_recv.at[i], ps_sem.at[i], pr_sem.at[i], wide=other)

    def final_copy(r):
        i = lax.rem(wide // 2 + r, half)
        return remote(final_send.at[i], final_recv.at[wide // 2], fs_sem.at[r], fr_sem.at[wide // 2],
                      wide=2 * i + side)

    @pl.loop(0, half)
    def _(r):
        i = lax.rem(wide // 2 + 1 + r, half)
        b = 2 * i + 1 - side
        pair_send[i, 0:blk, :] = up_acc[block(b), :].astype(BF16)
        pair_send[i, blk:, :] = down_acc[block(b), :].astype(BF16)
        pair_copy(i).start()

    @pl.loop(1, half)
    def _(r):
        i = lax.rem(wide // 2 + r, half)
        b = 2 * i + side
        pair_copy(i).wait_recv()
        final_send[i, 0:blk, :] = (up_acc[block(b), :] + pair_recv[i, 0:blk, :].astype(F32)).astype(BF16)
        final_send[i, blk:, :] = (down_acc[block(b), :] + pair_recv[i, blk:, :].astype(F32)).astype(BF16)
        final_copy(r).start()

    label_out[...] = label_acc[tile(wide), :]

    @pl.loop(1, nw)
    def _(r):
        src = lax.rem(wide + r, nw)
        remote(label_send.at[tile(src)], label_recv.at[tile(src)], hs_sem.at[r], hr_sem.at[src], wide=src).wait_recv()
        label_out[...] += label_recv[tile(src), :].astype(F32)

    mine = wide // 2
    pair_copy(mine).wait_recv()
    up_out[...] = up_acc[block(wide), :] + pair_recv[mine, 0:blk, :].astype(F32)
    down_out[...] = down_acc[block(wide), :] + pair_recv[mine, blk:, :].astype(F32)

    @pl.loop(1, half)
    def _(r):
        i = lax.rem(mine + r, half)
        remote(final_send.at[i], final_recv.at[i], fs_sem.at[r], fr_sem.at[i], wide=2 * i + side).wait_recv()
        up_out[...] += final_recv[i, 0:blk, :].astype(F32)
        down_out[...] += final_recv[i, blk:, :].astype(F32)

    low, high = me == 0, me == nn - 1
    drain(up_send, up_in, us_sem, ur_sem, high)
    drain(dn_send, dn_in, ds_sem, dr_sem, low)
    drain(up_send2, up_in2, us2_sem, ur2_sem, high)
    drain(dn_send2, dn_in2, ds2_sem, dr2_sem, low)

    @pl.loop(1, nw)
    def _(r):
        label_copy(r).wait_send()
        log_copy(r).wait_send()
        home_copy(r).wait_send()

    @pl.loop(1, nn)
    def _(r):
        @pl.loop(0, chunks)
        def _(c):
            stat_copy(r, c).wait_send()

    @pl.loop(0, half)
    def _(i):
        pair_copy(i).wait_send()

    @pl.loop(1, half)
    def _(r):
        final_copy(r).wait_send()


def expected_log(rank_ids, sampled):
    rank_float = rank_ids.astype(F32)
    return (
        jnp.log(F32(sampled))
        + jnp.log(jnp.log1p(1.0 / (rank_float + 1.0)))
        - jnp.log(jnp.log(F32(CATALOG) + 1.0))
    )


def local(documents, label_weight, sample_ids, positive_cols, up_weight, down_weight):
    nw, nn = lax.axis_size("wide"), lax.axis_size("narrow")
    lab, width = label_weight.shape
    rows = documents.shape[0]
    ff = up_weight.shape[1]
    per_doc = positive_cols.shape[1]
    chunks, pieces = rows // CHUNK, rows // PIECE
    columns = lab * nw
    blk, half = width // nw, nw // 2
    log_exp = jnp.broadcast_to(expected_log(sample_ids, columns * nn)[None, :], (8, lab))
    pos = positive_cols.reshape(chunks, CHUNK, per_doc).transpose(0, 2, 1)
    V = pltpu.VMEM
    dma = pltpu.SemaphoreType.DMA
    wide_rows = [V((rows, width), BF16)] * 4
    label_grad, up_grad, down_grad = pl.pallas_call(
        functools.partial(kernel, nw, nn, per_doc),
        out_shape=[
            jax.ShapeDtypeStruct((lab, width), F32),
            jax.ShapeDtypeStruct((blk, ff), F32),
            jax.ShapeDtypeStruct((blk, ff), F32),
        ],
        in_specs=[pl.BlockSpec(memory_space=pltpu.VMEM)] * 6,
        out_specs=[pl.BlockSpec(memory_space=pltpu.VMEM)] * 3,
        scratch_shapes=[
            V((columns, width), BF16), V((nw, 8, lab), F32), V((columns, lab), F32),
            V((rows, ff), BF16), V((rows, ff), F32), V((rows, width), F32), V((rows, width), BF16),
            V((chunks, columns, CHUNK), F32), V((columns, CHUNK), BF16),
            V((chunks, 8, CHUNK), F32), V((nn, chunks, 8, CHUNK), F32),
            *wide_rows, *wide_rows,
            V((rows, width), F32), V((rows, width), BF16),
            V((columns, width), F32), V((columns, width), BF16), V((columns, width), BF16),
            V((width, ff), F32), V((width, ff), F32),
            V((half, 2 * blk, ff), BF16), V((half, 2 * blk, ff), BF16),
            V((half, 2 * blk, ff), BF16), V((half, 2 * blk, ff), BF16),
            dma((nw,)), dma((nw,)), dma((nw,)), dma((nw,)), dma((nn, chunks)), dma((nn, chunks)),
            *[dma((pieces,))] * 8,
            dma((nw,)), dma((nw,)), dma((half,)), dma((half,)), dma((half,)), dma((half,)),
        ],
        compiler_params=pltpu.CompilerParams(
            collective_id=0, has_side_effects=True, vmem_limit_bytes=60 * 1024 * 1024
        ),
    )(documents, label_weight, log_exp, pos, up_weight, down_weight)
    return (label_grad, up_grad, down_grad.T)


def solution(mesh):
    in_specs = (
        P("wide", None),
        P(("wide", "narrow"), None),
        P(("wide", "narrow")),
        P("wide", None),
        P(None, "narrow"),
        P("narrow", None),
    )
    out_specs = (P(("wide", "narrow"), None), P("wide", "narrow"), P("narrow", "wide"))
    return jax.shard_map(local, mesh=mesh, in_specs=in_specs, out_specs=out_specs, check_vma=False)
```

```python
import functools

import jax
import jax.numpy as jnp
from jax import lax
from jax.experimental import pallas as pl
from jax.experimental.pallas import tpu as pltpu
from jax.sharding import PartitionSpec as P

CATALOG = 2812281
MESH = pl.DeviceIdType.MESH
F32 = jnp.float32
BF16 = jnp.bfloat16
CHUNK = 256
PIECE = 64
LAG = 3
STAT_LAG = 2
NN = (((1,), (0,)), ((), ()))
NT = (((1,), (1,)), ((), ()))
TN = (((0,), (0,)), ((), ()))


def dot(a, b, dims):
    return lax.dot_general(a, b, dims, preferred_element_type=F32)


def kernel(
    nw, nn, per_doc,
    docs, label, log_exp, pos, up, down,
    label_out, up_out, down_out,
    labels, log_all, log_col, hidden, slope, own, emb, expo, grad, stat, stat_all,
    up_in, up_send, dn_in, dn_send, up_in2, up_send2, dn_in2, dn_send2,
    own2, embed_grad, label_acc, label_send, label_recv, up_acc, down_acc, pair_send, pair_recv,
    final_send, final_recv,
    g_send, g_recv, l_send, l_recv, s_send, s_recv,
    us_sem, ur_sem, ds_sem, dr_sem, us2_sem, ur2_sem, ds2_sem, dr2_sem,
    hs_sem, hr_sem, ps_sem, pr_sem, fs_sem, fr_sem,
):
    rows = docs.shape[0]
    lab = label.shape[0]
    chunks, pieces = rows // CHUNK, rows // PIECE
    per_chunk = CHUNK // PIECE
    wide = lax.axis_index("wide")
    me = lax.axis_index("narrow")

    barrier = pltpu.get_barrier_semaphore()

    @pl.loop(1, nw)
    def _(r):
        pl.semaphore_signal(barrier, inc=1, device_id={"wide": lax.rem(wide + r, nw)}, device_id_type=MESH)

    @pl.loop(1, nn)
    def _(r):
        pl.semaphore_signal(barrier, inc=1, device_id={"narrow": lax.rem(me + r, nn)}, device_id_type=MESH)

    pl.semaphore_wait(barrier, nw + nn - 2)

    def remote(src, dst, send, recv, **device):
        return pltpu.make_async_remote_copy(
            src_ref=src, dst_ref=dst, send_sem=send, recv_sem=recv, device_id=device, device_id_type=MESH
        )

    def label_copy(r):
        return remote(label, labels.at[pl.ds(pl.multiple_of(wide * lab, lab), lab)], g_send.at[r], g_recv.at[wide],
                      wide=lax.rem(wide + r, nw))

    def log_copy(r):
        return remote(log_exp, log_all.at[wide], l_send.at[r], l_recv.at[wide], wide=lax.rem(wide + r, nw))

    @pl.loop(1, nw)
    def _(r):
        log_copy(r).start()
        label_copy(r).start()

    labels[pl.ds(pl.multiple_of(wide * lab, lab), lab), :] = label[...]
    log_all[wide] = log_exp[...]

    def chunk_of(c):
        return pl.ds(pl.multiple_of(c * CHUNK, CHUNK), CHUNK)

    def piece_of(p):
        return pl.ds(pl.multiple_of(p * PIECE, PIECE), PIECE)

    def forward(c):
        at = chunk_of(c)
        pre = dot(docs[at, :], up[...], NN)
        cdf = 0.5 * (1.0 + lax.erf(pre * 0.7071067811865476))
        slope[at, :] = cdf + pre * jnp.exp(-0.5 * pre * pre) * 0.3989422804014327
        mid = (pre * cdf).astype(BF16)
        hidden[at, :] = mid
        own[at, :] = dot(mid, down[...], NN)

    def scan_step(t, terms, u_in, u_send, d_in, d_send, us, ur, ds, dr, finish):
        def one(p, first, last, inbox, outbox, send, recv, target):
            at = piece_of(p)

            @pl.when((p >= 0) & (p < pieces))
            def _():
                @pl.when(jnp.logical_not(first))
                def _():
                    remote(outbox.at[at], inbox.at[at], send.at[p], recv.at[p], narrow=target).wait_recv()

                @pl.when(jnp.logical_not(last))
                def _():
                    @pl.when(first)
                    def _():
                        outbox[at, :] = terms[at, :].astype(BF16)

                    @pl.when(jnp.logical_not(first))
                    def _():
                        outbox[at, :] = (terms[at, :] + inbox[at, :].astype(F32)).astype(BF16)

                    remote(outbox.at[at], inbox.at[at], send.at[p], recv.at[p], narrow=target).start()

        low, high = me == 0, me == nn - 1
        one(t - LAG * me, low, high, u_in, u_send, us, ur, lax.rem(me + 1, nn))
        one(t - LAG * (nn - 1 - me), high, low, d_in, d_send, ds, dr, lax.rem(me + nn - 1, nn))
        q = t - LAG * jnp.maximum(me, nn - 1 - me)
        at = piece_of(q)

        @pl.when((q >= 0) & (q < pieces))
        def _():
            @pl.when(low)
            def _():
                finish(at, terms[at, :] + d_in[at, :].astype(F32))

            @pl.when(high)
            def _():
                finish(at, terms[at, :] + u_in[at, :].astype(F32))

            @pl.when(jnp.logical_not(low | high))
            def _():
                finish(at, terms[at, :] + u_in[at, :].astype(F32) + d_in[at, :].astype(F32))

        return q

    def drain(outbox, inbox, send, recv, skip):
        @pl.when(jnp.logical_not(skip))
        def _():
            @pl.loop(0, pieces)
            def _(p):
                at = piece_of(p)
                remote(outbox.at[at], inbox.at[at], send.at[p], recv.at[p], narrow=lax.rem(me + 1, nn)).wait_send()

    def when_chunk(q, act):
        done = (q >= 0) & (q < pieces) & (lax.rem(q + pieces, per_chunk) == per_chunk - 1)

        @pl.when(done)
        def _():
            act(q // per_chunk)

    def tile(w):
        return pl.ds(pl.multiple_of(w * lab, lab), lab)

    def stat_copy(r, c):
        return remote(stat.at[c], stat_all.at[me, c], s_send.at[r, c], s_recv.at[me, c], narrow=lax.rem(me + r, nn))

    def logits(c):
        @pl.when(c == 0)
        def _():
            @pl.loop(1, nw)
            def _(r):
                src = lax.rem(wide + r, nw)
                remote(label, labels.at[tile(src)], g_send.at[r], g_recv.at[src], wide=src).wait_recv()
                remote(log_exp, log_all.at[src], l_send.at[r], l_recv.at[src], wide=src).wait_recv()

            @pl.loop(0, nw)
            def _(w):
                log_col[tile(w), :] = jnp.broadcast_to(log_all[w][0:1, :], (lab, lab)).T

        expo[c] = dot(labels[...], emb[chunk_of(c), :], NT)

        def top(w, best):
            part = expo[c, tile(w), :] - log_col[tile(w), 0:1]
            expo[c, tile(w), :] = part
            return jnp.maximum(best, jnp.max(part, axis=0, keepdims=True))

        best = lax.fori_loop(0, nw, top, jnp.full((1, CHUNK), -jnp.inf, F32))

        def add(w, total):
            part = jnp.exp(expo[c, tile(w), :] - best)
            expo[c, tile(w), :] = part
            return total + jnp.sum(part, axis=0, keepdims=True)

        total = lax.fori_loop(0, nw, add, jnp.zeros((1, CHUNK), F32))
        stat[c, 0:1, :] = best
        stat[c, 1:2, :] = total

        @pl.loop(1, nn)
        def _(r):
            stat_copy(r, c).start()

    def finish_embedding(at, value):
        emb[at, :] = (docs[at, :].astype(F32) + value).astype(BF16)

    stat[...] = jnp.zeros_like(stat)
    forward(0)

    def gradient(c):
        @pl.loop(1, nn)
        def _(r):
            src = lax.rem(me + r, nn)
            remote(stat.at[c], stat_all.at[src, c], s_send.at[r, c], s_recv.at[src, c], narrow=src).wait_recv()

        mine, mine_sum = stat[c, 0:1, :], stat[c, 1:2, :]
        top = lax.fori_loop(
            1, nn, lambda r, m: jnp.maximum(m, stat_all[lax.rem(me + r, nn), c, 0:1, :]), mine
        )

        def add(r, s):
            src = lax.rem(me + r, nn)
            return s + stat_all[src, c, 1:2, :] * jnp.exp(stat_all[src, c, 0:1, :] - top)

        shrink = jnp.exp(mine - top)
        scale = shrink / lax.fori_loop(1, nn, add, mine_sum * shrink)
        offsets = lax.broadcasted_iota(jnp.int32, (lab, CHUNK), 0)

        @pl.loop(0, nw)
        def _(w):
            columns = offsets + (w * nn + me) * lab
            hits = jnp.zeros((lab, CHUNK), F32)
            for k in range(per_doc):
                hits = hits + jnp.where(pos[c, k : k + 1, :] == columns, 1.0, 0.0)
            grad[tile(w), :] = (expo[c, tile(w), :] * scale - hits / per_doc).astype(BF16)

        own2[chunk_of(c), :] = dot(grad[...], labels[...], TN)

    def label_part(c):
        label_acc[...] += dot(grad[...], emb[chunk_of(c), :], NN)

    def home_copy(r):
        to = lax.rem(wide + r, nw)
        return remote(label_send.at[tile(to)], label_recv.at[tile(wide)], hs_sem.at[r], hr_sem.at[wide], wide=to)

    def finish_gradient(at, value):
        embed_grad[at, :] = value.astype(BF16)

    def backward(c):
        at = chunk_of(c)
        back = embed_grad[at, :]
        pre_grad = (dot(back, down[...], NT) * slope[at, :]).astype(BF16)
        up_acc[...] += dot(docs[at, :], pre_grad, TN)
        down_acc[...] += dot(back, hidden[at, :], TN)

    label_acc[...] = jnp.zeros_like(label_acc)
    up_acc[...] = jnp.zeros_like(up_acc)
    down_acc[...] = jnp.zeros_like(down_acc)
    first_grad = per_chunk + LAG * (nn - 1) + STAT_LAG - 1
    second = first_grad + 1

    @pl.loop(0, second + pieces + LAG * (nn - 1))
    def _(t):
        q = scan_step(t, own, up_in, up_send, dn_in, dn_send, us_sem, ur_sem, ds_sem, dr_sem, finish_embedding)

        @pl.when(t < chunks - 1)
        def _():
            forward(t + 1)

        when_chunk(q, logits)
        q2 = scan_step(
            t - second, own2, up_in2, up_send2, dn_in2, dn_send2, us2_sem, ur2_sem, ds2_sem, dr2_sem,
            finish_gradient,
        )
        since = t - first_grad
        turn = lax.rem(since + pieces, per_chunk)

        @pl.when((since >= 0) & (since < pieces) & (turn == 0))
        def _():
            gradient(since // per_chunk)

        @pl.when((since >= 0) & (since < pieces) & (turn == 1))
        def _():
            label_part(since // per_chunk)

        @pl.when(since == pieces - per_chunk + 1)
        def _():
            label_send[...] = label_acc[...].astype(BF16)

            @pl.loop(1, nw)
            def _(r):
                home_copy(r).start()

        when_chunk(q2, backward)

    blk = up_acc.shape[0] // nw
    half = nw // 2
    side = lax.rem(wide, 2)
    other = wide + 1 - 2 * side

    def block(b):
        return pl.ds(pl.multiple_of(b * blk, blk), blk)

    def pair_copy(i):
        return remote(pair_send.at[i], pair_recv.at[i], ps_sem.at[i], pr_sem.at[i], wide=other)

    def final_copy(r):
        i = lax.rem(wide // 2 + r, half)
        return remote(final_send.at[i], final_recv.at[wide // 2], fs_sem.at[r], fr_sem.at[wide // 2],
                      wide=2 * i + side)

    @pl.loop(0, half)
    def _(r):
        i = lax.rem(wide // 2 + 1 + r, half)
        b = 2 * i + 1 - side
        pair_send[i, 0:blk, :] = up_acc[block(b), :].astype(BF16)
        pair_send[i, blk:, :] = down_acc[block(b), :].astype(BF16)
        pair_copy(i).start()

    @pl.loop(1, half)
    def _(r):
        i = lax.rem(wide // 2 + r, half)
        b = 2 * i + side
        pair_copy(i).wait_recv()
        final_send[i, 0:blk, :] = (up_acc[block(b), :] + pair_recv[i, 0:blk, :].astype(F32)).astype(BF16)
        final_send[i, blk:, :] = (down_acc[block(b), :] + pair_recv[i, blk:, :].astype(F32)).astype(BF16)
        final_copy(r).start()

    label_out[...] = label_acc[tile(wide), :]

    @pl.loop(1, nw)
    def _(r):
        src = lax.rem(wide + r, nw)
        remote(label_send.at[tile(src)], label_recv.at[tile(src)], hs_sem.at[r], hr_sem.at[src], wide=src).wait_recv()
        label_out[...] += label_recv[tile(src), :].astype(F32)

    mine = wide // 2
    pair_copy(mine).wait_recv()
    up_out[...] = up_acc[block(wide), :] + pair_recv[mine, 0:blk, :].astype(F32)
    down_out[...] = down_acc[block(wide), :] + pair_recv[mine, blk:, :].astype(F32)

    @pl.loop(1, half)
    def _(r):
        i = lax.rem(mine + r, half)
        remote(final_send.at[i], final_recv.at[i], fs_sem.at[r], fr_sem.at[i], wide=2 * i + side).wait_recv()
        up_out[...] += final_recv[i, 0:blk, :].astype(F32)
        down_out[...] += final_recv[i, blk:, :].astype(F32)

    low, high = me == 0, me == nn - 1
    drain(up_send, up_in, us_sem, ur_sem, high)
    drain(dn_send, dn_in, ds_sem, dr_sem, low)
    drain(up_send2, up_in2, us2_sem, ur2_sem, high)
    drain(dn_send2, dn_in2, ds2_sem, dr2_sem, low)

    @pl.loop(1, nw)
    def _(r):
        label_copy(r).wait_send()
        log_copy(r).wait_send()
        home_copy(r).wait_send()

    @pl.loop(1, nn)
    def _(r):
        @pl.loop(0, chunks)
        def _(c):
            stat_copy(r, c).wait_send()

    @pl.loop(0, half)
    def _(i):
        pair_copy(i).wait_send()

    @pl.loop(1, half)
    def _(r):
        final_copy(r).wait_send()


def expected_log(rank_ids, sampled):
    rank_float = rank_ids.astype(F32)
    return (
        jnp.log(F32(sampled))
        + jnp.log(jnp.log1p(1.0 / (rank_float + 1.0)))
        - jnp.log(jnp.log(F32(CATALOG) + 1.0))
    )


def local(documents, label_weight, sample_ids, positive_cols, up_weight, down_weight):
    nw, nn = lax.axis_size("wide"), lax.axis_size("narrow")
    lab, width = label_weight.shape
    rows = documents.shape[0]
    ff = up_weight.shape[1]
    per_doc = positive_cols.shape[1]
    chunks, pieces = rows // CHUNK, rows // PIECE
    columns = lab * nw
    blk, half = width // nw, nw // 2
    log_exp = jnp.broadcast_to(expected_log(sample_ids, columns * nn)[None, :], (8, lab))
    pos = positive_cols.reshape(chunks, CHUNK, per_doc).transpose(0, 2, 1)
    V = pltpu.VMEM
    dma = pltpu.SemaphoreType.DMA
    wide_rows = [V((rows, width), BF16)] * 4
    label_grad, up_grad, down_grad = pl.pallas_call(
        functools.partial(kernel, nw, nn, per_doc),
        out_shape=[
            jax.ShapeDtypeStruct((lab, width), F32),
            jax.ShapeDtypeStruct((blk, ff), F32),
            jax.ShapeDtypeStruct((blk, ff), F32),
        ],
        in_specs=[pl.BlockSpec(memory_space=pltpu.VMEM)] * 6,
        out_specs=[pl.BlockSpec(memory_space=pltpu.VMEM)] * 3,
        scratch_shapes=[
            V((columns, width), BF16), V((nw, 8, lab), F32), V((columns, lab), F32),
            V((rows, ff), BF16), V((rows, ff), F32), V((rows, width), F32), V((rows, width), BF16),
            V((chunks, columns, CHUNK), F32), V((columns, CHUNK), BF16),
            V((chunks, 8, CHUNK), F32), V((nn, chunks, 8, CHUNK), F32),
            *wide_rows, *wide_rows,
            V((rows, width), F32), V((rows, width), BF16),
            V((columns, width), F32), V((columns, width), BF16), V((columns, width), BF16),
            V((width, ff), F32), V((width, ff), F32),
            V((half, 2 * blk, ff), BF16), V((half, 2 * blk, ff), BF16),
            V((half, 2 * blk, ff), BF16), V((half, 2 * blk, ff), BF16),
            dma((nw,)), dma((nw,)), dma((nw,)), dma((nw,)), dma((nn, chunks)), dma((nn, chunks)),
            *[dma((pieces,))] * 8,
            dma((nw,)), dma((nw,)), dma((half,)), dma((half,)), dma((half,)), dma((half,)),
        ],
        compiler_params=pltpu.CompilerParams(
            collective_id=0, has_side_effects=True, vmem_limit_bytes=60 * 1024 * 1024
        ),
    )(documents, label_weight, log_exp, pos, up_weight, down_weight)
    return (label_grad, up_grad, down_grad.T)


def solution(mesh):
    in_specs = (
        P("wide", None),
        P(("wide", "narrow"), None),
        P(("wide", "narrow")),
        P("wide", None),
        P(None, "narrow"),
        P("narrow", None),
    )
    out_specs = (P(("wide", "narrow"), None), P("wide", "narrow"), P("narrow", "wide"))
    return jax.shard_map(local, mesh=mesh, in_specs=in_specs, out_specs=out_specs, check_vma=False)
```
